32 devices in a mesh: search: 16 (over z, y, x), mp: 2 (over core).
Axes of the slice: x: 2, y: 2, z: 4, core: 2. Of those that a mesh axis runs over, the one named last changes fastest.
Arguments:
- queries: bfloat16 [256, 2, 128, 192], P('search', None, 'mp'), may hold values from -240 to 240
- new_latents: bfloat16 [256, 2, 576], P('search'), may hold values from -6 to 6
- parent_cache: bfloat16 [16, 4096, 576], P('search'), may hold values from -4 to 4
- parent_of: int32 [256], P('search'), may hold values from 0 to 15, as said below
- up_keys: bfloat16 [128, 128, 512], P('mp'), may hold values from -0.5 to 0.5
- up_values: bfloat16 [128, 512, 128], P('mp'), may hold values from -0.25 to 0.25
- out_proj: bfloat16 [16384, 7168], P('mp', 'search'), may hold values from -0.0625 to 0.0625
- hidden_in: bfloat16 [256, 2, 7168], P('search', None, 'mp'), may hold values from -22 to 22
- router: bfloat16 [7168, 16], P('mp'), may hold values from -0.0625 to 0.0625
- routes: int32 [256, 2, 8], P('search'), may hold values from 0 to 15, all different within a row; in each aligned block of 32 rows (0 to 31, 32 to 63, ..., all dimensions but the last counted through in order) at most 24 rows name the same one
- w_gate: bfloat16 [16, 7168, 1024], P('search', None, 'mp'), may hold values from -0.0625 to 0.0625
- w_up: bfloat16 [16, 7168, 1024], P('search', None, 'mp'), may hold values from -0.0625 to 0.0625
- w_down: bfloat16 [16, 1024, 7168], P('search', 'mp'), may hold values from -0.25 to 0.25
Outputs:
- mixed: bfloat16 [256, 2, 7168], P('search', None, 'mp')
The draws below stay inside these ranges and needn't reach their ends.
Inputs may be any that keep to these rules, and one draw needn't show every extreme that they name: `parent_of`: the children of one device fall into 8 groups of 2 children with a common parent, the groups' parents all different; every parent has 16 children. `routes`: each row names 8 different experts; in the rows of one device no expert is named more than 24 times, and that most is reached.
All inputs are finite; a program needn't handle non-finite values.
Results may differ from the reference program's by a relative error of at most 0.017.
Values may be sent and summed in bfloat16 or wider, within the bound.
A program may use at most 192 MiB of HBM per device.

```python
import math
import jax
import jax.numpy as jnp
import numpy as np
from jax import lax

D = 7168
HEADS = 128
NOPE = 128
ROPE = 64
LATENT = 512
VDIM = 128
TOPK = 8
EXPERT_HIDDEN = 1024
NEW = 2
C_DEV = 16
PREFIX = 4096
CHILDREN = 256
PARENTS = 16
EXPERTS = 16
GROUPS = 8
KPAIR = 2
CAP = 24
N_SEARCH = 16
N_MP = 2


STRENGTHS = (120.0, 240.0, 380.0)


def parent_table(key):
    base = jax.random.fold_in(key, 101)
    first, second, third, fourth = jax.random.split(base, 4)
    shuffle_a = jax.random.permutation(first, N_SEARCH)
    shuffle_b = jax.random.permutation(second, N_SEARCH)
    offsets = jax.random.permutation(third, N_SEARCH)[:GROUPS]
    orders = jax.vmap(lambda member: jax.random.permutation(member, C_DEV))(jax.random.split(fourth, N_SEARCH))
    group_of = orders // KPAIR
    devices = jnp.arange(N_SEARCH)[:, None]
    target = shuffle_b[(shuffle_a[devices] + offsets[group_of]) % N_SEARCH]
    return target.reshape(CHILDREN).astype(jnp.int32)


def cache_parts(key):
    base = jax.random.fold_in(key, 202)
    first, second, third = jax.random.split(base, 3)
    latent_part = jnp.clip(jax.random.normal(first, (PARENTS, PREFIX, LATENT)), -4.0, 4.0)
    rope_part = jnp.clip(jax.random.normal(second, (PARENTS, PREFIX, ROPE)), -4.0, 4.0)
    anchor = jax.random.randint(third, (PARENTS,), 0, PREFIX - 1)
    strength = jnp.array(STRENGTHS, jnp.float32)[jnp.arange(PARENTS) % 3]
    anchor_key = rope_part[jnp.arange(PARENTS), anchor]
    return (latent_part, rope_part, anchor_key, strength)


def own_rope(key):
    return 1.5 * jnp.clip(jax.random.normal(jax.random.fold_in(key, 303), (CHILDREN, NEW, ROPE)), -4.0, 4.0)


def draw_parent_of(key, part):
    return parent_table(key)


def draw_parent_cache(key, part):
    parts = cache_parts(key)
    return jnp.concatenate([parts[0], parts[1]], axis=-1).astype(jnp.bfloat16)


def draw_new_latents(key, part):
    latent_key = jax.random.fold_in(key, 505)
    latent_part = jnp.clip(jax.random.normal(latent_key, (CHILDREN, NEW, LATENT)), -4.0, 4.0)
    return jnp.concatenate([latent_part, own_rope(key)], axis=-1).astype(jnp.bfloat16)


def draw_queries(key, part):
    base = jax.random.fold_in(key, 404)
    first, second = jax.random.split(base, 2)
    nope_part = jnp.clip(jax.random.normal(first, (CHILDREN, NEW, HEADS, NOPE)), -4.0, 4.0)
    noise = jnp.clip(jax.random.normal(second, (CHILDREN, NEW, HEADS, ROPE)), -4.0, 4.0)
    own_keys = own_rope(key)
    shared = own_keys[:, 0] + own_keys[:, 1]
    rope_part = 0.6 * shared[:, None, None, :] + 0.5 * noise
    return jnp.concatenate([nope_part, rope_part], axis=-1).astype(jnp.bfloat16)


def draw_hidden_in(key, part):
    base = jax.random.fold_in(key, 606)
    first, second = jax.random.split(base, 2)
    row_scale = jnp.exp(jax.random.uniform(second, (CHILDREN, NEW, 1), minval=math.log(0.3), maxval=math.log(3.0)))
    ramp = jnp.arange(D, dtype=jnp.float32) / D
    values = jnp.clip(jax.random.normal(first, (CHILDREN, NEW, D)), -4.0, 4.0)
    column_scale = 3.0 ** ramp / 1.7
    return (values * row_scale * column_scale).astype(jnp.bfloat16)


def raised(values, own_key, source, target, blocks, factor):
    def block_of(dim):
        return (jnp.arange(values.shape[dim]) // (values.shape[dim] // blocks)).reshape((-1,) + (1,) * (values.ndim - 1 - dim))

    first = jax.random.permutation(own_key, blocks)[block_of(target)]
    second = (block_of(target) + blocks // 2) % blocks
    return jnp.where((block_of(source) == first) | (block_of(source) == second), factor * values, values)


def steps_of(key, dims, shards, smallest, high):
    def one(axis_at, shards_of):
        heights = jax.random.uniform(jax.random.fold_in(jax.random.fold_in(key, 6), axis_at), (shards_of,), jnp.float32, smallest / len(shards), high / len(shards))
        return jnp.repeat(jnp.exp(heights), dims[axis_at] // shards_of).reshape((-1,) + (1,) * (len(dims) - axis_at - 1))

    factor_of = one(*shards[0])
    for cut in shards[1:]:
        factor_of = factor_of * one(*cut)
    return factor_of


def assign_block(own_key, own, number, rows, count, top, bound, slope):
    ranking = jax.random.permutation(own_key, count)
    crowded, usual = load_shares(count, rows * top, bound, slope, True), load_shares(count, rows * top, bound, slope, False)
    places = jnp.arange(count)

    def named(tallies, rotation):
        used = int((tallies > 0).sum())
        fixed = max(1, used // 4)
        shifted = fixed + (places - fixed + rotation * (used - fixed)) % max(1, count - fixed)
        return jnp.zeros((count,), jnp.int32).at[ranking[jnp.where(places < fixed, places, shifted)]].set(jnp.asarray(tallies, jnp.int32))

    tallies = jnp.where(number % 4 == 0, named(crowded, number // 4), named(usual, number - number // 4 - 1))
    mixed = jax.random.permutation(jax.random.fold_in(own, 3), count)
    giver, receiver = mixed[0:count // 2 * 2:2], mixed[1:count // 2 * 2:2]
    slack = jnp.minimum(tallies[giver] - 1, bound - tallies[receiver]) // 2
    slack = jnp.where((giver == ranking[0]) | (receiver == ranking[0]) | (tallies[receiver] == 0), 0, jnp.maximum(slack, 0))
    shifted = jax.random.randint(jax.random.fold_in(own, 4), (count // 2,), 0, 1 << 20) % (slack + 1)
    tallies = tallies.at[giver].add(-shifted).at[receiver].add(shifted)
    items = jnp.searchsorted(jnp.cumsum(tallies), jnp.arange(rows * top), side="right").astype(jnp.int32)
    grid = items.reshape(top, rows).T
    grid = grid[jax.random.permutation(jax.random.fold_in(own, 1), rows)]
    rotation = jax.random.randint(jax.random.fold_in(own, 2), (rows, 1), 0, top)
    return jnp.take_along_axis(grid, (jnp.arange(top)[None, :] + rotation) % top, axis=1)


def load_shares(count, total, limit, lean, full):
    portions = [(1 << 20) // math.isqrt(standing ** lean) + 1 for standing in range(1, count + 1)]
    largest = limit if full else min(limit, max(-(-total // count), total * portions[0] // sum(portions)))
    least = 1 if total - largest >= count - 1 else 0
    counts, spare = [largest] + [least] * (count - 1), total - largest - least * (count - 1)
    while spare > 0:
        candidates = [i for i in range(1, count) if counts[i] < largest] or [i for i in range(1, count) if counts[i] < limit]
        whole, remaining = sum([portions[i] for i in candidates]), spare
        for i in candidates:
            more = min(limit - counts[i], max(1, remaining * portions[i] // whole), spare)
            counts[i] = counts[i] + more
            spare = spare - more
    return np.array(counts)


def normal_values(stream_key, shape, spread, bound, cuts=(), kind=jnp.bfloat16):
    loudness = steps_of(stream_key, shape, cuts, -0.22, 0.18) if cuts else 1.0
    values = jax.random.normal(stream_key, shape, jnp.float32) * spread * loudness
    return jnp.minimum(jnp.maximum(values, -bound), bound).astype(kind)


def noise_with(key, extent, width, most, shards, heavy, kind=jnp.bfloat16):
    drawn = width * jax.random.normal(key, extent, jnp.float32)
    if shards:
        drawn = drawn * steps_of(key, extent, shards, -0.22, 0.18)
    return jnp.clip(raised(drawn, jax.random.fold_in(key, 3), *heavy), -most, most).astype(kind)


def setup_inputs(seed: int = 0) -> dict:
    key_list = jax.random.split(jax.random.key(seed), 14)
    queries = draw_queries(jax.random.fold_in(key_list[13], 71), 0)
    new_latents = draw_new_latents(jax.random.fold_in(key_list[13], 71), 0)
    parent_cache = draw_parent_cache(jax.random.fold_in(key_list[13], 71), 0)
    parent_of = draw_parent_of(jax.random.fold_in(key_list[13], 71), 0)
    up_keys = normal_values(key_list[4], (HEADS, NOPE, LATENT), NOPE ** -0.5, 0.5, ((0, 2),))
    up_values = normal_values(key_list[5], (HEADS, LATENT, VDIM), LATENT ** -0.5, 0.25, ((0, 2),))
    out_proj = noise_with(key_list[6], (HEADS * VDIM, D), (HEADS * VDIM) ** -0.5, 0.0625, ((0, 2), (1, 16)), (0, 1, 16, 2.0))
    hidden_in = draw_hidden_in(jax.random.fold_in(key_list[13], 71), 0)
    router = normal_values(key_list[8], (D, EXPERTS), D ** -0.5, 0.0625, ((0, 2),))
    routes_keys = jax.random.split(jax.random.fold_in(key_list[9], 1), CHILDREN * NEW // (C_DEV * NEW))
    routes_turns = jax.random.permutation(jax.random.fold_in(key_list[9], 3), CHILDREN * NEW // (C_DEV * NEW))
    routes = jax.vmap(lambda own, number: assign_block(jax.random.fold_in(key_list[9], 2), own, number, C_DEV * NEW, EXPERTS, TOPK, CAP, 2))(routes_keys, routes_turns).reshape((CHILDREN, NEW, TOPK))
    w_gate = normal_values(key_list[10], (EXPERTS, D, EXPERT_HIDDEN), D ** -0.5, 0.0625, ((0, 16), (2, 2)))
    w_up = normal_values(key_list[11], (EXPERTS, D, EXPERT_HIDDEN), D ** -0.5, 0.0625, ((0, 16), (2, 2)))
    w_down = noise_with(key_list[12], (EXPERTS, EXPERT_HIDDEN, D), EXPERT_HIDDEN ** -0.5, 0.25, ((0, 16), (1, 2)), (1, 2, 2, 2.0))
    return {"queries": queries, "new_latents": new_latents, "parent_cache": parent_cache, "parent_of": parent_of, "up_keys": up_keys, "up_values": up_values, "out_proj": out_proj, "hidden_in": hidden_in, "router": router, "routes": routes, "w_gate": w_gate, "w_up": w_up, "w_down": w_down}


def attend_child(query_block, own_keys, prefix_cache, up_keys, up_values):
    softmax_scale = (NOPE + ROPE) ** (-0.5)
    latent_query = jnp.einsum('thn,hnl->thl', query_block[..., :NOPE].astype(jnp.float32), up_keys.astype(jnp.float32)).astype(jnp.bfloat16)
    full_query = jnp.concatenate([latent_query, query_block[..., NOPE:]], axis=-1)
    all_keys = jnp.concatenate([prefix_cache, own_keys], axis=0)
    scores = jnp.dot(full_query.reshape(NEW * HEADS, LATENT + ROPE), all_keys.T, preferred_element_type=jnp.float32) * softmax_scale
    scores = scores.reshape(NEW, HEADS, PREFIX + NEW)
    token_pos = jnp.arange(NEW, dtype=jnp.int32)[:, None]
    key_pos = jnp.arange(PREFIX + NEW, dtype=jnp.int32)[None, :]
    visible = key_pos < PREFIX + token_pos + 1
    scores = jnp.where(visible[:, None, :], scores, -jnp.inf)
    row_peak = lax.optimization_barrier(jnp.max(scores, axis=-1, keepdims=True))
    weights = jnp.exp(scores - row_peak)
    row_mass = lax.optimization_barrier(jnp.sum(weights, axis=-1, keepdims=True))
    summed = jnp.dot(weights.astype(jnp.bfloat16).reshape(NEW * HEADS, PREFIX + NEW), all_keys[:, :LATENT], preferred_element_type=jnp.float32)
    latent_out = (summed.reshape(NEW, HEADS, LATENT) / row_mass).astype(jnp.bfloat16)
    head_out = jnp.einsum('thl,hlv->thv', latent_out.astype(jnp.float32), up_values.astype(jnp.float32)).astype(jnp.bfloat16)
    return head_out.reshape(NEW, HEADS * VDIM)

def reference(queries, new_latents, parent_cache, parent_of, up_keys, up_values, out_proj, hidden_in, router, routes, w_gate, w_up, w_down):

    def one_child(child_index):
        prefix_cache = parent_cache[parent_of[child_index]]
        return attend_child(queries[child_index], new_latents[child_index], prefix_cache, up_keys, up_values)
    attention = lax.map(one_child, jnp.arange(CHILDREN, dtype=jnp.int32))
    token_count = CHILDREN * NEW
    attention = attention.reshape(token_count, HEADS * VDIM)
    residual = (hidden_in.reshape(token_count, D).astype(jnp.float32) + jnp.dot(attention, out_proj, preferred_element_type=jnp.float32)).astype(jnp.bfloat16)
    residual_wide = residual.astype(jnp.float32)
    inv_rms = lax.rsqrt(lax.optimization_barrier(jnp.mean(residual_wide * residual_wide, axis=1)) + 1e-06)
    logits = jnp.dot(residual, router, preferred_element_type=jnp.float32) * inv_rms[:, None]
    normed = (residual_wide * inv_rms[:, None]).astype(jnp.bfloat16)
    picked = routes.reshape(token_count, TOPK)
    affinity = jax.nn.sigmoid(logits)
    chosen = jnp.take_along_axis(affinity, picked, axis=1)
    gate_weights = 2.5 * chosen / lax.optimization_barrier(jnp.sum(chosen, axis=1, keepdims=True))
    part_width = EXPERT_HIDDEN // N_MP
    slot_limit = N_SEARCH * CAP

    def one_expert(expert_mix, expert):
        matches = picked == expert
        weight_row = lax.optimization_barrier(jnp.sum(jnp.where(matches, gate_weights, 0.0), axis=1))
        selected = jnp.any(matches, axis=1)
        row_index = jnp.nonzero(selected, size=slot_limit, fill_value=0)[0]
        live_slot = jnp.arange(slot_limit) < jnp.sum(selected)
        inputs = normed[row_index]
        gate_act = jnp.dot(inputs, w_gate[expert], preferred_element_type=jnp.float32)
        up_act = jnp.dot(inputs, w_up[expert], preferred_element_type=jnp.float32)
        expert_hidden = (jax.nn.silu(gate_act) * up_act).astype(jnp.bfloat16)
        partials = jnp.einsum('smk,mkd->msd', expert_hidden.reshape(slot_limit, N_MP, part_width).astype(jnp.float32), w_down[expert].reshape(N_MP, part_width, D).astype(jnp.float32)).astype(jnp.bfloat16)
        expert_out = lax.optimization_barrier(jnp.sum(partials.astype(jnp.float32), axis=0))
        row_scale = jnp.where(live_slot, weight_row[row_index], 0.0)
        return (expert_mix.at[row_index].add(expert_out * row_scale[:, None]), None)
    expert_mix, unused = lax.scan(one_expert, jnp.zeros((token_count, D), jnp.float32), jnp.arange(EXPERTS, dtype=jnp.int32))
    mixed = (residual_wide + expert_mix).astype(jnp.bfloat16)
    return mixed.reshape(CHILDREN, NEW, D)
```

```python
import functools

import jax
import jax.numpy as jnp
from jax import lax
from jax.experimental import pallas as pl
from jax.experimental.pallas import tpu as pltpu
from jax.sharding import PartitionSpec as P

D = 7168
BF16, F32, I32 = jnp.bfloat16, jnp.float32, jnp.int32


def attend_kernel(tile_children, heads, softmax_scale, latent_width, key_chunk,
                  query_ref, own_ref, cache_ref, out_ref, scores_ref):
    rows = query_ref.shape[0]
    prefix = cache_ref.shape[0]
    query = query_ref[...]
    nt = (((1,), (1,)), ((), ()))
    own = own_ref[...]
    own_count = own.shape[0]
    own_scores = lax.dot_general(query, own, nt, preferred_element_type=F32) * softmax_scale
    row_id = lax.broadcasted_iota(I32, (rows, own_count), 0) // heads
    key_id = lax.broadcasted_iota(I32, (rows, own_count), 1)
    steps = own_count // tile_children
    visible = (row_id // steps == key_id // steps) & (key_id % steps <= row_id % steps)
    own_scores = jnp.where(visible, own_scores, -jnp.inf)
    peak = jnp.max(own_scores, axis=1, keepdims=True)
    for start in range(0, prefix, key_chunk):
        chunk = lax.dot_general(
            query, cache_ref[pl.ds(start, key_chunk), :], nt, preferred_element_type=F32
        ) * softmax_scale
        scores_ref[:, pl.ds(start, key_chunk)] = chunk
        peak = jnp.maximum(peak, jnp.max(chunk, axis=1, keepdims=True))
    own_weights = jnp.exp(own_scores - peak)
    mass = jnp.sum(own_weights, axis=1, keepdims=True)
    total = jnp.dot(own_weights.astype(BF16), own[:, :latent_width], preferred_element_type=F32)
    for start in range(0, prefix, key_chunk):
        weights = jnp.exp(scores_ref[:, pl.ds(start, key_chunk)] - peak)
        mass = mass + jnp.sum(weights, axis=1, keepdims=True)
        total = total + jnp.dot(
            weights.astype(BF16),
            cache_ref[pl.ds(start, key_chunk), :latent_width],
            preferred_element_type=F32,
        )
    out_ref[...] = (total / mass).astype(BF16)


def attend(full_query, own_latents, prefix_cache, latent_width, softmax_scale):
    children, steps, heads, kv_width = full_query.shape
    tile_children = max(1, min(children, 512 // (steps * heads)))
    rows = tile_children * steps * heads
    prefix = prefix_cache.shape[0]
    tiles = children // tile_children
    body = functools.partial(attend_kernel, tile_children, heads, softmax_scale, latent_width, min(1024, prefix))
    own_rows = tile_children * steps
    own_tiles = own_latents.reshape(tiles, own_rows, kv_width)
    out = pl.pallas_call(
        body,
        grid=(tiles,),
        in_specs=[
            pl.BlockSpec((rows, kv_width), lambda i: (i, 0)),
            pl.BlockSpec((pl.squeezed, own_rows, kv_width), lambda i: (i, 0, 0)),
            pl.BlockSpec((prefix, kv_width), lambda i: (0, 0)),
        ],
        out_specs=pl.BlockSpec((rows, latent_width), lambda i: (i, 0)),
        out_shape=jax.ShapeDtypeStruct((tiles * rows, latent_width), BF16),
        scratch_shapes=[pltpu.VMEM((rows, prefix), F32)],
        compiler_params=pltpu.CompilerParams(vmem_limit_bytes=52 * 1024 * 1024),
        cost_estimate=pl.CostEstimate(
            flops=2 * tiles * rows * prefix * (kv_width + latent_width),
            bytes_accessed=2 * (tiles * rows * (kv_width + latent_width) + prefix * kv_width),
            transcendentals=tiles * rows * prefix,
        ),
        name="attend",
    )(full_query.reshape(tiles * rows, kv_width), own_tiles, prefix_cache)
    return out.reshape(children, steps, heads, latent_width)


def local(
    queries,
    new_latents,
    parent_cache,
    parent_of,
    up_keys,
    up_values,
    out_proj,
    hidden_in,
    router,
    routes,
    w_gate,
    w_up,
    w_down,
):
    searchers = lax.axis_size("search")
    me = lax.axis_index("search")
    children_here, new_tokens, heads_here, query_width = queries.shape
    nope_width = up_keys.shape[1]
    latent_width = up_keys.shape[2]
    kv_width = parent_cache.shape[2]
    value_width = up_values.shape[2]
    softmax_scale = float(query_width) ** (-0.5)
    pair_slots = children_here // (searchers // 2)
    children_all = searchers * children_here
    token_rows = children_here * new_tokens
    width_here = hidden_in.shape[2]

    parents = lax.all_gather(parent_of, "search", axis=0, tiled=True)
    ids = jnp.arange(children_all, dtype=I32)
    earlier_same = (parents[:, None] == parents[None, :]) & (ids[None, :] < ids[:, None])
    ranking = jnp.sum(earlier_same.astype(I32), axis=1)
    same_device = (ids[:, None] // children_here) == (ids[None, :] // children_here)
    pair_rank = jnp.sum((earlier_same & same_device).astype(I32), axis=1)
    position = parents * children_here + ranking
    arrival_slot = (ids // children_here) * pair_slots + pair_rank
    slots_total = searchers * pair_slots
    mine = me * children_here + jnp.arange(children_here, dtype=I32)
    taken = mine[:, None] == position[None, :]
    slot_of_mine = jnp.sum(jnp.where(taken, arrival_slot[None, :], 0), axis=1)
    picker = (slot_of_mine[:, None] == jnp.arange(slots_total, dtype=I32)[None, :]).astype(BF16)

    own_ids = jnp.arange(children_here, dtype=I32)
    own_rank = jnp.sum(
        ((parent_of[:, None] == parent_of[None, :]) & (own_ids[None, :] < own_ids[:, None])).astype(I32), axis=1
    )
    own_slot = parent_of * pair_slots + own_rank
    placer = (jnp.arange(slots_total, dtype=I32)[:, None] == own_slot[None, :]).astype(BF16)

    query_cols = new_tokens * heads_here * query_width
    payload = jnp.concatenate(
        [queries.reshape(children_here, -1), new_latents.reshape(children_here, -1)], axis=1
    )
    outgoing = jnp.dot(placer, payload, preferred_element_type=F32).astype(BF16)
    arrived = lax.all_to_all(outgoing, "search", split_axis=0, concat_axis=0, tiled=True)
    held = jnp.dot(picker, arrived, preferred_element_type=F32).astype(BF16)
    held_query = held[:, :query_cols].reshape(children_here, new_tokens, heads_here, query_width)
    held_latents = held[:, query_cols:].reshape(children_here, new_tokens, kv_width)

    latent_query = jnp.einsum(
        "cthn,hnl->cthl", held_query[..., :nope_width], up_keys, preferred_element_type=F32
    ).astype(BF16)
    full_query = jnp.concatenate([latent_query, held_query[..., nope_width:]], axis=-1)
    latent_out = attend(full_query, held_latents, parent_cache[0], latent_width, softmax_scale)
    head_out = jnp.einsum("cthl,hlv->cthv", latent_out, up_values, preferred_element_type=F32).astype(BF16)
    attention = head_out.reshape(token_rows, heads_here * value_width)

    gathered = lax.all_gather(attention, "search", axis=0, tiled=True)
    every_row = jnp.dot(gathered, out_proj, preferred_element_type=F32).astype(BF16)
    column_block = every_row.shape[1]
    every_row = jnp.take(
        every_row.reshape(children_all, new_tokens * column_block), position, axis=0
    ).reshape(children_all * new_tokens, column_block)
    owned = lax.all_to_all(every_row, "search", split_axis=0, concat_axis=1, tiled=True)
    projected = lax.psum_scatter(owned, "mp", scatter_dimension=1, tiled=True).astype(F32)
    residual = (hidden_in.reshape(token_rows, width_here).astype(F32) + projected).astype(BF16)
    residual_wide = residual.astype(F32)
    squares = jnp.sum(residual_wide * residual_wide, axis=1)
    router_part = jnp.dot(residual, router, preferred_element_type=F32)
    squares, router_part = lax.psum((squares, router_part), "mp")
    inv_rms = lax.rsqrt(squares / D + 1e-06)
    logits = router_part * inv_rms[:, None]
    normed = (residual_wide * inv_rms[:, None]).astype(BF16)

    experts_total = router.shape[1]
    picked = routes.reshape(token_rows, -1)
    affinity = jax.nn.sigmoid(logits)
    chosen_mask = jnp.any(picked[:, :, None] == jnp.arange(experts_total, dtype=I32)[None, None, :], axis=1)
    chosen = jnp.where(chosen_mask, affinity, 0.0)
    gates = 2.5 * chosen / jnp.sum(chosen, axis=1, keepdims=True)

    all_gates = lax.all_gather(gates, "search", axis=0, tiled=True)
    my_gate = jnp.sum(
        jnp.where(jnp.arange(experts_total, dtype=I32)[None, :] == me, all_gates, 0.0), axis=1
    )
    slices = lax.all_gather(normed, "search", axis=0, tiled=True)
    tokens = lax.all_gather(slices, "mp", axis=1, tiled=True)
    gate_act = jnp.dot(tokens, w_gate[0], preferred_element_type=F32)
    up_act = jnp.dot(tokens, w_up[0], preferred_element_type=F32)
    expert_hidden = (jax.nn.silu(gate_act) * up_act).astype(BF16)
    expert_part = jnp.dot(expert_hidden, w_down[0], preferred_element_type=F32)
    weighted = (expert_part * my_gate[:, None]).astype(BF16)
    weighted = lax.psum_scatter(weighted, "mp", scatter_dimension=1, tiled=True)
    expert_mix = lax.psum_scatter(weighted, "search", scatter_dimension=0, tiled=True).astype(F32)
    mixed = (residual_wide + expert_mix).astype(BF16)
    return mixed.reshape(children_here, new_tokens, width_here)


def solution(mesh):
    in_specs = (
        P("search", None, "mp", None),
        P("search", None, None),
        P("search", None, None),
        P("search"),
        P("mp", None, None),
        P("mp", None, None),
        P("mp", "search"),
        P("search", None, "mp"),
        P("mp", None),
        P("search", None, None),
        P("search", None, "mp"),
        P("search", None, "mp"),
        P("search", "mp", None),
    )
    out_specs = P("search", None, "mp")
    return jax.shard_map(local, mesh=mesh, in_specs=in_specs, out_specs=out_specs, check_vma=False)
```

```python
import functools

import jax
import jax.numpy as jnp
from jax import lax
from jax.experimental import pallas as pl
from jax.experimental.pallas import tpu as pltpu
from jax.sharding import PartitionSpec as P

D = 7168
BF16, F32, I32 = jnp.bfloat16, jnp.float32, jnp.int32


def attend_kernel(tile_children, heads, softmax_scale, latent_width, key_chunk,
                  query_ref, own_ref, cache_ref, out_ref, scores_ref):
    rows = query_ref.shape[0]
    prefix = cache_ref.shape[0]
    query = query_ref[...]
    nt = (((1,), (1,)), ((), ()))
    own = own_ref[...]
    own_count = own.shape[0]
    own_scores = lax.dot_general(query, own, nt, preferred_element_type=F32) * softmax_scale
    row_id = lax.broadcasted_iota(I32, (rows, own_count), 0) // heads
    key_id = lax.broadcasted_iota(I32, (rows, own_count), 1)
    steps = own_count // tile_children
    visible = (row_id // steps == key_id // steps) & (key_id % steps <= row_id % steps)
    own_scores = jnp.where(visible, own_scores, -jnp.inf)
    peak = jnp.max(own_scores, axis=1, keepdims=True)
    for start in range(0, prefix, key_chunk):
        chunk = lax.dot_general(
            query, cache_ref[pl.ds(start, key_chunk), :], nt, preferred_element_type=F32
        ) * softmax_scale
        scores_ref[:, pl.ds(start, key_chunk)] = chunk
        peak = jnp.maximum(peak, jnp.max(chunk, axis=1, keepdims=True))
    own_weights = jnp.exp(own_scores - peak)
    mass = jnp.sum(own_weights, axis=1, keepdims=True)
    total = jnp.dot(own_weights.astype(BF16), own[:, :latent_width], preferred_element_type=F32)
    for start in range(0, prefix, key_chunk):
        weights = jnp.exp(scores_ref[:, pl.ds(start, key_chunk)] - peak)
        mass = mass + jnp.sum(weights, axis=1, keepdims=True)
        total = total + jnp.dot(
            weights.astype(BF16),
            cache_ref[pl.ds(start, key_chunk), :latent_width],
            preferred_element_type=F32,
        )
    out_ref[...] = (total / mass).astype(BF16)


def attend(full_query, own_latents, prefix_cache, latent_width, softmax_scale):
    children, steps, heads, kv_width = full_query.shape
    tile_children = max(1, min(children, 512 // (steps * heads)))
    rows = tile_children * steps * heads
    prefix = prefix_cache.shape[0]
    tiles = children // tile_children
    body = functools.partial(attend_kernel, tile_children, heads, softmax_scale, latent_width, min(1024, prefix))
    own_rows = tile_children * steps
    own_tiles = own_latents.reshape(tiles, own_rows, kv_width)
    out = pl.pallas_call(
        body,
        grid=(tiles,),
        in_specs=[
            pl.BlockSpec((rows, kv_width), lambda i: (i, 0)),
            pl.BlockSpec((pl.squeezed, own_rows, kv_width), lambda i: (i, 0, 0)),
            pl.BlockSpec((prefix, kv_width), lambda i: (0, 0)),
        ],
        out_specs=pl.BlockSpec((rows, latent_width), lambda i: (i, 0)),
        out_shape=jax.ShapeDtypeStruct((tiles * rows, latent_width), BF16),
        scratch_shapes=[pltpu.VMEM((rows, prefix), F32)],
        compiler_params=pltpu.CompilerParams(vmem_limit_bytes=52 * 1024 * 1024),
        cost_estimate=pl.CostEstimate(
            flops=2 * tiles * rows * prefix * (kv_width + latent_width),
            bytes_accessed=2 * (tiles * rows * (kv_width + latent_width) + prefix * kv_width),
            transcendentals=tiles * rows * prefix,
        ),
        name="attend",
    )(full_query.reshape(tiles * rows, kv_width), own_tiles, prefix_cache)
    return out.reshape(children, steps, heads, latent_width)


def gather_kernel(across, x_ref, o_ref, send_sem, recv_sem, core_send, core_recv, local_sem):
    me, core = lax.axis_index("search"), lax.axis_index("mp")
    x, y, z = lax.rem(me, 2), lax.rem(lax.div(me, 2), 2), lax.div(me, 4)
    half = x_ref.shape[0] // 2

    def at(zz, yy, xx):
        return (zz * 2 + yy) * 2 + xx

    x_peer, y_peer, above, below = at(z, y, 1 - x), at(z, 1 - y, x), me + 4, me - 4
    has_above, has_below = z < 3, z > 0

    def block(item):
        return o_ref.at[core, item] if across else o_ref.at[item]

    def remote(src, dst, sent, landed, device):
        return pltpu.make_async_remote_copy(
            src_ref=src, dst_ref=dst, send_sem=sent, recv_sem=landed,
            device_id=device, device_id_type=pl.DeviceIdType.MESH,
        )

    def send(kind, landing, zc, item, target, src=None, rows=None):
        dst = block(item) if rows is None else block(item).at[rows]
        return remote(dst if src is None else src, dst, send_sem.at[kind, zc], recv_sem.at[landing, zc],
                      (target, core))

    def to_core(item, src=None):
        return remote(block(item) if src is None else src, block(item), core_send.at[item], core_recv.at[item],
                      (me, 1 - core))

    def share(item, src=None):
        if across:
            to_core(item, src).start()

    low, high = pl.ds(0, half), pl.ds(half, half)
    barrier = pltpu.get_barrier_semaphore()

    def greet(device):
        pl.semaphore_signal(barrier, inc=1, device_id=device, device_id_type=pl.DeviceIdType.MESH)

    greet((x_peer, core))
    greet((y_peer, core))
    if across:
        greet((me, 1 - core))

    @pl.when(has_above)
    def _():
        greet((above, core))

    @pl.when(has_below)
    def _():
        greet((below, core))

    pl.semaphore_wait(barrier, (4 if across else 3) + lax.div(z * (3 - z), 2))

    def spread(zc, src=None):
        item = at(zc, y, x)
        send(2, 1, zc, item, x_peer, src).start()
        send(3, 2, zc, item, y_peer, src).start()

    def climb(zc, src=None):
        @pl.when(has_above)
        def _():
            send(0, 0, zc, at(zc, y, x), above, src).start()

    def descend(zc, src=None):
        @pl.when(has_below)
        def _():
            send(1, 0, zc, at(zc, y, x), below, src).start()

    def relay(zc):
        from_x, from_y = at(zc, y, 1 - x), at(zc, 1 - y, x)
        send(2, 1, zc, from_x, x_peer).wait_recv()
        send(5, 4, zc, from_x, y_peer, rows=low).start()
        send(3, 2, zc, from_y, y_peer).wait_recv()
        send(4, 3, zc, from_y, x_peer, rows=high).start()
        share(from_x)
        share(from_y)

    climb(z, x_ref)
    descend(z, x_ref)
    spread(z, x_ref)
    share(me, x_ref)
    own = pltpu.make_async_copy(x_ref, block(me), local_sem)
    own.start()
    for k in range(1, 4):
        @pl.when(z >= k)
        def _():
            zc = z - k
            send(0, 0, zc, at(zc, y, x), above).wait_recv()
            climb(zc)
            spread(zc)
            share(at(zc, y, x))

        @pl.when(z + k < 4)
        def _():
            zc = z + k
            send(0, 0, zc, at(zc, y, x), above).wait_recv()
            descend(zc)
            spread(zc)
            share(at(zc, y, x))

        if k == 1:
            relay(z)
        else:
            @pl.when(z >= k - 1)
            def _():
                relay(z - (k - 1))

            @pl.when(z + k - 1 < 4)
            def _():
                relay(z + (k - 1))

    @pl.when(z >= 3)
    def _():
        relay(z - 3)

    @pl.when(z + 3 < 4)
    def _():
        relay(z + 3)

    for zc in range(4):
        diagonal = at(zc, 1 - y, 1 - x)
        send(5, 4, zc, diagonal, y_peer, rows=low).wait_recv()
        send(4, 3, zc, diagonal, x_peer, rows=high).wait_recv()
        share(diagonal)
    for zc in range(4):
        @pl.when((z >= zc) & has_above)
        def _():
            send(0, 0, zc, at(zc, y, x), above).wait_send()

        @pl.when((z <= zc) & has_below)
        def _():
            send(1, 0, zc, at(zc, y, x), below).wait_send()

        send(2, 1, zc, at(zc, y, x), x_peer).wait_send()
        send(3, 2, zc, at(zc, y, x), y_peer).wait_send()
        send(4, 3, zc, at(zc, 1 - y, x), x_peer, rows=high).wait_send()
        send(5, 4, zc, at(zc, y, 1 - x), y_peer, rows=low).wait_send()
    own.wait()
    if across:
        for item in range(16):
            to_core(item).wait_send()
            remote(o_ref.at[1 - core, item], o_ref.at[1 - core, item], core_send.at[item], core_recv.at[item],
                   (me, 1 - core)).wait_recv()


def gather_blocks(block, across, collective_id):
    shape = ((2, 16) if across else (16,)) + block.shape
    return pl.pallas_call(
        functools.partial(gather_kernel, across),
        out_shape=jax.ShapeDtypeStruct(shape, block.dtype),
        in_specs=[pl.BlockSpec(memory_space=pl.ANY)],
        out_specs=pl.BlockSpec(memory_space=pl.ANY),
        scratch_shapes=[
            pltpu.SemaphoreType.DMA((6, 4)),
            pltpu.SemaphoreType.DMA((5, 4)),
            pltpu.SemaphoreType.DMA((16,)),
            pltpu.SemaphoreType.DMA((16,)),
            pltpu.SemaphoreType.DMA,
        ],
        compiler_params=pltpu.CompilerParams(collective_id=collective_id, has_side_effects=True),
        name="gather_tokens" if across else "gather_heads",
    )(block)


def fold(values, axis, distance):
    count = lax.axis_size("search")
    bit = lax.rem(lax.div(lax.axis_index("search"), distance), 2)
    keep = lax.dynamic_index_in_dim(values, bit, axis, keepdims=False)
    give = lax.dynamic_index_in_dim(values, 1 - bit, axis, keepdims=False)
    got = lax.ppermute(give, "search", [(i, i ^ distance) for i in range(count)])
    return (keep.astype(F32) + got.astype(F32)).astype(values.dtype)


def scatter_sum(values, rows):
    width = values.shape[1]
    split = values.reshape(2, 2, 2, 2, rows, width)
    first, second = split[..., : width // 2], split[..., width // 2:]
    first = fold(fold(first, 3, 1), 2, 2)
    second = fold(fold(second, 2, 2), 2, 1)
    both = jnp.concatenate([first, second], axis=-1)
    return fold(fold(both, 1, 4), 0, 8)


def local(
    queries,
    new_latents,
    parent_cache,
    parent_of,
    up_keys,
    up_values,
    out_proj,
    hidden_in,
    router,
    routes,
    w_gate,
    w_up,
    w_down,
):
    searchers = lax.axis_size("search")
    me = lax.axis_index("search")
    children_here, new_tokens, heads_here, query_width = queries.shape
    nope_width = up_keys.shape[1]
    latent_width = up_keys.shape[2]
    kv_width = parent_cache.shape[2]
    value_width = up_values.shape[2]
    softmax_scale = float(query_width) ** (-0.5)
    pair_slots = children_here // (searchers // 2)
    children_all = searchers * children_here
    token_rows = children_here * new_tokens
    width_here = hidden_in.shape[2]

    parents = lax.all_gather(parent_of, "search", axis=0, tiled=True)
    ids = jnp.arange(children_all, dtype=I32)
    earlier_same = (parents[:, None] == parents[None, :]) & (ids[None, :] < ids[:, None])
    ranking = jnp.sum(earlier_same.astype(I32), axis=1)
    same_device = (ids[:, None] // children_here) == (ids[None, :] // children_here)
    pair_rank = jnp.sum((earlier_same & same_device).astype(I32), axis=1)
    position = parents * children_here + ranking
    arrival_slot = (ids // children_here) * pair_slots + pair_rank
    slots_total = searchers * pair_slots
    mine = me * children_here + jnp.arange(children_here, dtype=I32)
    taken = mine[:, None] == position[None, :]
    slot_of_mine = jnp.sum(jnp.where(taken, arrival_slot[None, :], 0), axis=1)
    picker = (slot_of_mine[:, None] == jnp.arange(slots_total, dtype=I32)[None, :]).astype(BF16)

    own_ids = jnp.arange(children_here, dtype=I32)
    own_rank = jnp.sum(
        ((parent_of[:, None] == parent_of[None, :]) & (own_ids[None, :] < own_ids[:, None])).astype(I32), axis=1
    )
    own_slot = parent_of * pair_slots + own_rank
    placer = (jnp.arange(slots_total, dtype=I32)[:, None] == own_slot[None, :]).astype(BF16)

    query_cols = new_tokens * heads_here * query_width
    payload = jnp.concatenate(
        [queries.reshape(children_here, -1), new_latents.reshape(children_here, -1)], axis=1
    )
    outgoing = jnp.dot(placer, payload, preferred_element_type=F32).astype(BF16)
    arrived = lax.all_to_all(outgoing, "search", split_axis=0, concat_axis=0, tiled=True)
    held = jnp.dot(picker, arrived, preferred_element_type=F32).astype(BF16)
    held_query = held[:, :query_cols].reshape(children_here, new_tokens, heads_here, query_width)
    held_latents = held[:, query_cols:].reshape(children_here, new_tokens, kv_width)

    latent_query = jnp.einsum(
        "cthn,hnl->cthl", held_query[..., :nope_width], up_keys, preferred_element_type=F32
    ).astype(BF16)
    full_query = jnp.concatenate([latent_query, held_query[..., nope_width:]], axis=-1)
    latent_out = attend(full_query, held_latents, parent_cache[0], latent_width, softmax_scale)
    head_out = jnp.einsum("cthl,hlv->cthv", latent_out, up_values, preferred_element_type=F32).astype(BF16)
    attention = head_out.reshape(token_rows, heads_here * value_width)

    block_4x2x2 = searchers == 16 and lax.axis_size("mp") == 2
    if block_4x2x2:
        gathered = gather_blocks(attention, False, 0).reshape(searchers * token_rows, -1)
    else:
        gathered = lax.all_gather(attention, "search", axis=0, tiled=True)
    every_row = jnp.dot(gathered, out_proj, preferred_element_type=F32).astype(BF16)
    column_block = every_row.shape[1]
    every_row = jnp.take(
        every_row.reshape(children_all, new_tokens * column_block), position, axis=0
    ).reshape(children_all * new_tokens, column_block)
    owned = lax.all_to_all(every_row, "search", split_axis=0, concat_axis=1, tiled=True)
    projected = lax.psum_scatter(owned, "mp", scatter_dimension=1, tiled=True).astype(F32)
    residual = (hidden_in.reshape(token_rows, width_here).astype(F32) + projected).astype(BF16)
    residual_wide = residual.astype(F32)
    squares = jnp.sum(residual_wide * residual_wide, axis=1)
    router_part = jnp.dot(residual, router, preferred_element_type=F32)
    squares, router_part = lax.psum((squares, router_part), "mp")
    inv_rms = lax.rsqrt(squares / D + 1e-06)
    logits = router_part * inv_rms[:, None]
    normed = (residual_wide * inv_rms[:, None]).astype(BF16)

    experts_total = router.shape[1]
    picked = routes.reshape(token_rows, -1)
    affinity = jax.nn.sigmoid(logits)
    chosen_mask = jnp.any(picked[:, :, None] == jnp.arange(experts_total, dtype=I32)[None, None, :], axis=1)
    chosen = jnp.where(chosen_mask, affinity, 0.0)
    gates = 2.5 * chosen / jnp.sum(chosen, axis=1, keepdims=True)

    if block_4x2x2:
        gates_high = gates.astype(BF16)
        gates_low = (gates - gates_high.astype(F32)).astype(BF16)
        spare = jnp.zeros((token_rows, 128 - 2 * experts_total), BF16)
        block = jnp.concatenate([normed, gates_high, gates_low, spare], axis=1)
        slices = gather_blocks(block, True, 1).reshape(2, searchers * token_rows, width_here + 128)
        sent = slices[0, :, width_here:].astype(F32)
        all_gates = sent[:, :experts_total] + sent[:, experts_total : 2 * experts_total]
        slices = [slices[part, :, :width_here] for part in range(2)]
    else:
        all_gates = lax.all_gather(gates, "search", axis=0, tiled=True)
        slices = lax.all_gather(normed, "search", axis=0, tiled=True)
        slices = lax.all_gather(slices, "mp", axis=0)
    my_gate = jnp.sum(
        jnp.where(jnp.arange(experts_total, dtype=I32)[None, :] == me, all_gates, 0.0), axis=1
    )
    gate_act, up_act = 0.0, 0.0
    for part in range(len(slices)):
        span = slice(part * width_here, (part + 1) * width_here)
        gate_act += jnp.dot(slices[part], w_gate[0, span], preferred_element_type=F32)
        up_act += jnp.dot(slices[part], w_up[0, span], preferred_element_type=F32)
    expert_hidden = (jax.nn.silu(gate_act) * up_act).astype(BF16)
    expert_part = jnp.dot(expert_hidden, w_down[0], preferred_element_type=F32)
    weighted = (expert_part * my_gate[:, None]).astype(BF16)
    weighted = lax.psum_scatter(weighted, "mp", scatter_dimension=1, tiled=True)
    if block_4x2x2:
        expert_mix = scatter_sum(weighted, token_rows).astype(F32)
    else:
        expert_mix = lax.psum_scatter(weighted, "search", scatter_dimension=0, tiled=True).astype(F32)
    mixed = (residual_wide + expert_mix).astype(BF16)
    return mixed.reshape(children_here, new_tokens, width_here)


def solution(mesh):
    in_specs = (
        P("search", None, "mp", None),
        P("search", None, None),
        P("search", None, None),
        P("search"),
        P("mp", None, None),
        P("mp", None, None),
        P("mp", "search"),
        P("search", None, "mp"),
        P("mp", None),
        P("search", None, None),
        P("search", None, "mp"),
        P("search", None, "mp"),
        P("search", "mp", None),
    )
    out_specs = P("search", None, "mp")
    return jax.shard_map(local, mesh=mesh, in_specs=in_specs, out_specs=out_specs, check_vma=False)
```

```python
import functools

import jax
import jax.numpy as jnp
from jax import lax
from jax.experimental import pallas as pl
from jax.experimental.pallas import tpu as pltpu
from jax.sharding import PartitionSpec as P

D = 7168
BF16, F32, I32 = jnp.bfloat16, jnp.float32, jnp.int32


def attend_kernel(tile_children, heads, softmax_scale, latent_width, key_chunk,
                  query_ref, own_ref, cache_ref, out_ref, scores_ref):
    rows = query_ref.shape[0]
    prefix = cache_ref.shape[0]
    query = query_ref[...]
    nt = (((1,), (1,)), ((), ()))
    own = own_ref[...]
    own_count = own.shape[0]
    own_scores = lax.dot_general(query, own, nt, preferred_element_type=F32) * softmax_scale
    row_id = lax.broadcasted_iota(I32, (rows, own_count), 0) // heads
    key_id = lax.broadcasted_iota(I32, (rows, own_count), 1)
    steps = own_count // tile_children
    visible = (row_id // steps == key_id // steps) & (key_id % steps <= row_id % steps)
    own_scores = jnp.where(visible, own_scores, -jnp.inf)
    peak = jnp.max(own_scores, axis=1, keepdims=True)
    for start in range(0, prefix, key_chunk):
        chunk = lax.dot_general(
            query, cache_ref[pl.ds(start, key_chunk), :], nt, preferred_element_type=F32
        ) * softmax_scale
        scores_ref[:, pl.ds(start, key_chunk)] = chunk
        peak = jnp.maximum(peak, jnp.max(chunk, axis=1, keepdims=True))
    own_weights = jnp.exp(own_scores - peak)
    mass = jnp.sum(own_weights, axis=1, keepdims=True)
    total = jnp.dot(own_weights.astype(BF16), own[:, :latent_width], preferred_element_type=F32)
    for start in range(0, prefix, key_chunk):
        weights = jnp.exp(scores_ref[:, pl.ds(start, key_chunk)] - peak)
        mass = mass + jnp.sum(weights, axis=1, keepdims=True)
        total = total + jnp.dot(
            weights.astype(BF16),
            cache_ref[pl.ds(start, key_chunk), :latent_width],
            preferred_element_type=F32,
        )
    out_ref[...] = (total / mass).astype(BF16)


def attend(full_query, own_latents, prefix_cache, latent_width, softmax_scale):
    children, steps, heads, kv_width = full_query.shape
    tile_children = max(1, min(children, 512 // (steps * heads)))
    rows = tile_children * steps * heads
    prefix = prefix_cache.shape[0]
    tiles = children // tile_children
    body = functools.partial(attend_kernel, tile_children, heads, softmax_scale, latent_width, min(1024, prefix))
    own_rows = tile_children * steps
    own_tiles = own_latents.reshape(tiles, own_rows, kv_width)
    out = pl.pallas_call(
        body,
        grid=(tiles,),
        in_specs=[
            pl.BlockSpec((rows, kv_width), lambda i: (i, 0)),
            pl.BlockSpec((pl.squeezed, own_rows, kv_width), lambda i: (i, 0, 0)),
            pl.BlockSpec((prefix, kv_width), lambda i: (0, 0)),
        ],
        out_specs=pl.BlockSpec((rows, latent_width), lambda i: (i, 0)),
        out_shape=jax.ShapeDtypeStruct((tiles * rows, latent_width), BF16),
        scratch_shapes=[pltpu.VMEM((rows, prefix), F32)],
        compiler_params=pltpu.CompilerParams(vmem_limit_bytes=52 * 1024 * 1024),
        cost_estimate=pl.CostEstimate(
            flops=2 * tiles * rows * prefix * (kv_width + latent_width),
            bytes_accessed=2 * (tiles * rows * (kv_width + latent_width) + prefix * kv_width),
            transcendentals=tiles * rows * prefix,
        ),
        name="attend",
    )(full_query.reshape(tiles * rows, kv_width), own_tiles, prefix_cache)
    return out.reshape(children, steps, heads, latent_width)


def gather_kernel(across, x_ref, o_ref, send_sem, recv_sem, core_send, core_recv, local_sem):
    me, core = lax.axis_index("search"), lax.axis_index("mp")
    x, y, z = lax.rem(me, 2), lax.rem(lax.div(me, 2), 2), lax.div(me, 4)
    half = x_ref.shape[0] // 2

    def at(zz, yy, xx):
        return (zz * 2 + yy) * 2 + xx

    x_peer, y_peer, above, below = at(z, y, 1 - x), at(z, 1 - y, x), me + 4, me - 4
    has_above, has_below = z < 3, z > 0

    def block(item):
        return o_ref.at[core, item] if across else o_ref.at[item]

    def remote(src, dst, sent, landed, device):
        return pltpu.make_async_remote_copy(
            src_ref=src, dst_ref=dst, send_sem=sent, recv_sem=landed,
            device_id=device, device_id_type=pl.DeviceIdType.MESH,
        )

    def send(kind, landing, zc, item, target, src=None, rows=None):
        dst = block(item) if rows is None else block(item).at[rows]
        return remote(dst if src is None else src, dst, send_sem.at[kind, zc], recv_sem.at[landing, zc],
                      (target, core))

    def to_core(item, src=None):
        return remote(block(item) if src is None else src, block(item), core_send.at[item], core_recv.at[item],
                      (me, 1 - core))

    def share(item, src=None):
        if across:
            to_core(item, src).start()

    low, high = pl.ds(0, half), pl.ds(half, half)
    barrier = pltpu.get_barrier_semaphore()

    def greet(device):
        pl.semaphore_signal(barrier, inc=1, device_id=device, device_id_type=pl.DeviceIdType.MESH)

    greet((x_peer, core))
    greet((y_peer, core))
    if across:
        greet((me, 1 - core))

    @pl.when(has_above)
    def _():
        greet((above, core))

    @pl.when(has_below)
    def _():
        greet((below, core))

    pl.semaphore_wait(barrier, (4 if across else 3) + lax.div(z * (3 - z), 2))

    def spread(zc, src=None):
        item = at(zc, y, x)
        send(2, 1, zc, item, x_peer, src).start()
        send(3, 2, zc, item, y_peer, src).start()

    def climb(zc, src=None):
        @pl.when(has_above)
        def _():
            send(0, 0, zc, at(zc, y, x), above, src).start()

    def descend(zc, src=None):
        @pl.when(has_below)
        def _():
            send(1, 0, zc, at(zc, y, x), below, src).start()

    def relay(zc):
        from_x, from_y = at(zc, y, 1 - x), at(zc, 1 - y, x)
        send(2, 1, zc, from_x, x_peer).wait_recv()
        send(5, 4, zc, from_x, y_peer, rows=low).start()
        send(3, 2, zc, from_y, y_peer).wait_recv()
        send(4, 3, zc, from_y, x_peer, rows=high).start()
        share(from_x)
        share(from_y)

    climb(z, x_ref)
    descend(z, x_ref)
    spread(z, x_ref)
    share(me, x_ref)
    own = pltpu.make_async_copy(x_ref, block(me), local_sem)
    own.start()
    for k in range(1, 4):
        @pl.when(z >= k)
        def _():
            zc = z - k
            send(0, 0, zc, at(zc, y, x), above).wait_recv()
            climb(zc)
            spread(zc)
            share(at(zc, y, x))

        @pl.when(z + k < 4)
        def _():
            zc = z + k
            send(0, 0, zc, at(zc, y, x), above).wait_recv()
            descend(zc)
            spread(zc)
            share(at(zc, y, x))

        if k == 1:
            relay(z)
        else:
            @pl.when(z >= k - 1)
            def _():
                relay(z - (k - 1))

            @pl.when(z + k - 1 < 4)
            def _():
                relay(z + (k - 1))

    @pl.when(z >= 3)
    def _():
        relay(z - 3)

    @pl.when(z + 3 < 4)
    def _():
        relay(z + 3)

    for zc in range(4):
        diagonal = at(zc, 1 - y, 1 - x)
        send(5, 4, zc, diagonal, y_peer, rows=low).wait_recv()
        send(4, 3, zc, diagonal, x_peer, rows=high).wait_recv()
        share(diagonal)
    for zc in range(4):
        @pl.when((z >= zc) & has_above)
        def _():
            send(0, 0, zc, at(zc, y, x), above).wait_send()

        @pl.when((z <= zc) & has_below)
        def _():
            send(1, 0, zc, at(zc, y, x), below).wait_send()

        send(2, 1, zc, at(zc, y, x), x_peer).wait_send()
        send(3, 2, zc, at(zc, y, x), y_peer).wait_send()
        send(4, 3, zc, at(zc, 1 - y, x), x_peer, rows=high).wait_send()
        send(5, 4, zc, at(zc, y, 1 - x), y_peer, rows=low).wait_send()
    own.wait()
    if across:
        for item in range(16):
            to_core(item).wait_send()
            remote(o_ref.at[1 - core, item], o_ref.at[1 - core, item], core_send.at[item], core_recv.at[item],
                   (me, 1 - core)).wait_recv()


def gather_blocks(block, across, collective_id):
    shape = ((2, 16) if across else (16,)) + block.shape
    return pl.pallas_call(
        functools.partial(gather_kernel, across),
        out_shape=jax.ShapeDtypeStruct(shape, block.dtype),
        in_specs=[pl.BlockSpec(memory_space=pl.ANY)],
        out_specs=pl.BlockSpec(memory_space=pl.ANY),
        scratch_shapes=[
            pltpu.SemaphoreType.DMA((6, 4)),
            pltpu.SemaphoreType.DMA((5, 4)),
            pltpu.SemaphoreType.DMA((16,)),
            pltpu.SemaphoreType.DMA((16,)),
            pltpu.SemaphoreType.DMA,
        ],
        compiler_params=pltpu.CompilerParams(collective_id=collective_id, has_side_effects=True),
        name="gather_tokens" if across else "gather_heads",
    )(block)


def fold(values, axis, distance):
    count = lax.axis_size("search")
    bit = lax.rem(lax.div(lax.axis_index("search"), distance), 2)
    keep = lax.dynamic_index_in_dim(values, bit, axis, keepdims=False)
    give = lax.dynamic_index_in_dim(values, 1 - bit, axis, keepdims=False)
    got = lax.ppermute(give, "search", [(i, i ^ distance) for i in range(count)])
    return (keep.astype(F32) + got.astype(F32)).astype(values.dtype)


def scatter_experts(hidden, weight, gate, rows):
    core = lax.axis_index("mp")
    width = weight.shape[1] // 2
    last = 2 * width // 7
    size = (width - last) // 2

    def product(owner, start, count):
        columns = lax.dynamic_slice_in_dim(weight, owner * width + start, count, 1)
        return (jnp.dot(hidden, columns, preferred_element_type=F32) * gate[:, None]).astype(BF16)

    def summed(start, count):
        got = lax.ppermute(product(1 - core, start, count), "mp", [(0, 1), (1, 0)])
        kept = product(core, start, count)
        total = (kept.astype(F32) + got.astype(F32)).astype(BF16)
        return total.reshape(2, 2, 2, 2, rows, count)

    third = summed(2 * size, last)
    first = summed(0, size)
    second = summed(size, size)
    third = fold(fold(third, 1, 4), 0, 8)
    first = fold(fold(first, 3, 1), 2, 2)
    second = fold(fold(second, 2, 2), 2, 1)
    third = fold(fold(third, 1, 1), 0, 2)
    both = jnp.concatenate([first, second], axis=-1)
    both = fold(fold(both, 1, 4), 0, 8)
    return jnp.concatenate([both, third], axis=-1)


def local(
    queries,
    new_latents,
    parent_cache,
    parent_of,
    up_keys,
    up_values,
    out_proj,
    hidden_in,
    router,
    routes,
    w_gate,
    w_up,
    w_down,
):
    searchers = lax.axis_size("search")
    me = lax.axis_index("search")
    children_here, new_tokens, heads_here, query_width = queries.shape
    nope_width = up_keys.shape[1]
    latent_width = up_keys.shape[2]
    kv_width = parent_cache.shape[2]
    value_width = up_values.shape[2]
    softmax_scale = float(query_width) ** (-0.5)
    pair_slots = children_here // (searchers // 2)
    children_all = searchers * children_here
    token_rows = children_here * new_tokens
    width_here = hidden_in.shape[2]

    parents = lax.all_gather(parent_of, "search", axis=0, tiled=True)
    ids = jnp.arange(children_all, dtype=I32)
    earlier_same = (parents[:, None] == parents[None, :]) & (ids[None, :] < ids[:, None])
    ranking = jnp.sum(earlier_same.astype(I32), axis=1)
    same_device = (ids[:, None] // children_here) == (ids[None, :] // children_here)
    pair_rank = jnp.sum((earlier_same & same_device).astype(I32), axis=1)
    position = parents * children_here + ranking
    arrival_slot = (ids // children_here) * pair_slots + pair_rank
    slots_total = searchers * pair_slots
    mine = me * children_here + jnp.arange(children_here, dtype=I32)
    taken = mine[:, None] == position[None, :]
    slot_of_mine = jnp.sum(jnp.where(taken, arrival_slot[None, :], 0), axis=1)
    picker = (slot_of_mine[:, None] == jnp.arange(slots_total, dtype=I32)[None, :]).astype(BF16)

    own_ids = jnp.arange(children_here, dtype=I32)
    own_rank = jnp.sum(
        ((parent_of[:, None] == parent_of[None, :]) & (own_ids[None, :] < own_ids[:, None])).astype(I32), axis=1
    )
    own_slot = parent_of * pair_slots + own_rank
    placer = (jnp.arange(slots_total, dtype=I32)[:, None] == own_slot[None, :]).astype(BF16)

    heads_part = heads_here // 2
    query_cols = new_tokens * heads_part * query_width
    head_outs, arrived, held_latents = [], None, None
    for part in range(2):
        heads = slice(part * heads_part, (part + 1) * heads_part)
        payload = queries[:, :, heads].reshape(children_here, -1)
        if part == 0:
            payload = jnp.concatenate([payload, new_latents.reshape(children_here, -1)], axis=1)
        outgoing = jnp.dot(placer, payload, preferred_element_type=F32).astype(BF16)
        if part == 1:
            outgoing, arrived = lax.optimization_barrier((outgoing, arrived))
        arrived = lax.all_to_all(outgoing, "search", split_axis=0, concat_axis=0, tiled=True)
        held = jnp.dot(picker, arrived, preferred_element_type=F32).astype(BF16)
        held_query = held[:, :query_cols].reshape(children_here, new_tokens, heads_part, query_width)
        if part == 0:
            held_latents = held[:, query_cols:].reshape(children_here, new_tokens, kv_width)
        latent_query = jnp.einsum(
            "cthn,hnl->cthl", held_query[..., :nope_width], up_keys[heads], preferred_element_type=F32
        ).astype(BF16)
        full_query = jnp.concatenate([latent_query, held_query[..., nope_width:]], axis=-1)
        latent_out = attend(full_query, held_latents, parent_cache[0], latent_width, softmax_scale)
        head_outs.append(
            jnp.einsum(
                "cthl,hlv->cthv", latent_out, up_values[heads], preferred_element_type=F32
            ).astype(BF16)
        )
    head_out = jnp.concatenate(head_outs, axis=2)
    attention = head_out.reshape(token_rows, heads_here * value_width)

    block_4x2x2 = searchers == 16 and lax.axis_size("mp") == 2
    if block_4x2x2:
        gathered = gather_blocks(attention, False, 0).reshape(searchers * token_rows, -1)
    else:
        gathered = lax.all_gather(attention, "search", axis=0, tiled=True)
    every_row = jnp.dot(gathered, out_proj, preferred_element_type=F32).astype(BF16)
    column_block = every_row.shape[1]
    every_row = jnp.take(
        every_row.reshape(children_all, new_tokens * column_block), position, axis=0
    ).reshape(children_all * new_tokens, column_block)
    owned = lax.all_to_all(every_row, "search", split_axis=0, concat_axis=1, tiled=True)
    projected = lax.psum_scatter(owned, "mp", scatter_dimension=1, tiled=True).astype(F32)
    residual = (hidden_in.reshape(token_rows, width_here).astype(F32) + projected).astype(BF16)
    residual_wide = residual.astype(F32)
    squares = jnp.sum(residual_wide * residual_wide, axis=1)
    router_part = jnp.dot(residual, router, preferred_element_type=F32)
    squares, router_part = lax.psum((squares, router_part), "mp")
    inv_rms = lax.rsqrt(squares / D + 1e-06)
    logits = router_part * inv_rms[:, None]
    normed = (residual_wide * inv_rms[:, None]).astype(BF16)

    experts_total = router.shape[1]
    picked = routes.reshape(token_rows, -1)
    affinity = jax.nn.sigmoid(logits)
    chosen_mask = jnp.any(picked[:, :, None] == jnp.arange(experts_total, dtype=I32)[None, None, :], axis=1)
    chosen = jnp.where(chosen_mask, affinity, 0.0)
    gates = 2.5 * chosen / jnp.sum(chosen, axis=1, keepdims=True)

    if block_4x2x2:
        gates_high = gates.astype(BF16)
        gates_low = (gates - gates_high.astype(F32)).astype(BF16)
        spare = jnp.zeros((token_rows, 128 - 2 * experts_total), BF16)
        block = jnp.concatenate([normed, gates_high, gates_low, spare], axis=1)
        slices = gather_blocks(block, True, 1).reshape(2, searchers * token_rows, width_here + 128)
        sent = slices[0, :, width_here:].astype(F32)
        all_gates = sent[:, :experts_total] + sent[:, experts_total : 2 * experts_total]
        slices = [slices[part, :, :width_here] for part in range(2)]
    else:
        all_gates = lax.all_gather(gates, "search", axis=0, tiled=True)
        slices = lax.all_gather(normed, "search", axis=0, tiled=True)
        slices = lax.all_gather(slices, "mp", axis=0)
    my_gate = jnp.sum(
        jnp.where(jnp.arange(experts_total, dtype=I32)[None, :] == me, all_gates, 0.0), axis=1
    )
    gate_act, up_act = 0.0, 0.0
    for part in range(len(slices)):
        span = slice(part * width_here, (part + 1) * width_here)
        gate_act += jnp.dot(slices[part], w_gate[0, span], preferred_element_type=F32)
        up_act += jnp.dot(slices[part], w_up[0, span], preferred_element_type=F32)
    expert_hidden = (jax.nn.silu(gate_act) * up_act).astype(BF16)
    if block_4x2x2:
        expert_mix = scatter_experts(expert_hidden, w_down[0], my_gate, token_rows).astype(F32)
    else:
        expert_part = jnp.dot(expert_hidden, w_down[0], preferred_element_type=F32)
        weighted = (expert_part * my_gate[:, None]).astype(BF16)
        weighted = lax.psum_scatter(weighted, "mp", scatter_dimension=1, tiled=True)
        expert_mix = lax.psum_scatter(weighted, "search", scatter_dimension=0, tiled=True).astype(F32)
    mixed = (residual_wide + expert_mix).astype(BF16)
    return mixed.reshape(children_here, new_tokens, width_here)


def solution(mesh):
    in_specs = (
        P("search", None, "mp", None),
        P("search", None, None),
        P("search", None, None),
        P("search"),
        P("mp", None, None),
        P("mp", None, None),
        P("mp", "search"),
        P("search", None, "mp"),
        P("mp", None),
        P("search", None, None),
        P("search", None, "mp"),
        P("search", None, "mp"),
        P("search", "mp", None),
    )
    out_specs = P("search", None, "mp")
    return jax.shard_map(local, mesh=mesh, in_specs=in_specs, out_specs=out_specs, check_vma=False)
```
